512 devices in a mesh: dp: 32 (over z, core), fsdp: 16 (over y, x).
Axes of the slice: x: 4, y: 4, z: 16, core: 2. Of those that a mesh axis runs over, the one named last changes fastest.
Arguments:
- tile: bfloat16 [65536, 2048], P(('dp', 'fsdp')), may hold values from -6 to 6
- cotangent: bfloat16 [65536, 2048], P(('dp', 'fsdp')), may hold values from -6 to 6
- combine: float32 [65536], P(('dp', 'fsdp')), may hold values from 0.05 to 0.6
- valid: int32 [512], P(('dp', 'fsdp')), may hold values from 1 to 128, as said below
- w_gate: bfloat16 [2048, 768], P('fsdp'), may hold values from -0.125 to 0.125
- w_up: bfloat16 [2048, 768], P('fsdp'), may hold values from -0.125 to 0.125
- w_down: bfloat16 [768, 2048], P(None, 'fsdp'), may hold values from -0.21875 to 0.21875
Outputs:
- output: bfloat16 [65536, 2048], P(('dp', 'fsdp'))
- tile_grad: bfloat16 [65536, 2048], P(('dp', 'fsdp'))
- combine_grad: float32 [65536], P(('dp', 'fsdp'))
- grad_gate: float32 [2048, 768], P('fsdp', 'dp')
- grad_up: float32 [2048, 768], P('fsdp', 'dp')
- grad_down: float32 [768, 2048], P('dp', 'fsdp')
The draws below stay inside these ranges and needn't reach their ends.
Inputs may be any that keep to these rules, and one draw needn't show every extreme that they name: `valid`: some device's tile is full in every draw.
All inputs are finite; a program needn't handle non-finite values.
Results may differ from the reference program's by a relative error of at most 0.0058.
Values may be sent and summed in bfloat16 or wider, within the bound.
A program may use at most 64 MiB of HBM per device.

```python
import jax
import jax.numpy as jnp
from jax import lax

D = 2048
FF = 768
CAP = 128
ROWS = 65536
DEVICES_ALL = 512


def draw_valid(key, part):
    key = jax.random.fold_in(key, 11)
    first, second = jax.random.split(key)
    levels = jax.random.randint(first, (DEVICES_ALL,), 1, 9)
    counts = jnp.maximum(CAP * levels // 8, 1)
    chosen = jax.random.randint(second, (), 0, DEVICES_ALL)
    counts = jnp.where(jnp.arange(DEVICES_ALL) == chosen, CAP, counts)
    return counts.astype(jnp.int32)


def block_scale(stream_key, shape, cuts, least, largest):
    factor_of, own = 1.0, jax.random.fold_in(stream_key, 6)
    for axis_at, shards_of in cuts:
        draws = jnp.exp(jax.random.uniform(jax.random.fold_in(own, axis_at), (shards_of,), jnp.float32, least / len(cuts), largest / len(cuts)))
        factor_of = factor_of * jnp.repeat(draws, shape[axis_at] // shards_of).reshape([-1 if axis == axis_at else 1 for axis in range(len(shape))])
    return factor_of


def centred(rng, dims, spread, reach, cuts=(), kind=jnp.bfloat16):
    result = jax.random.normal(rng, dims, jnp.float32) * spread
    if len(cuts) > 0:
        result = block_scale(rng, dims, cuts, -0.22, 0.18) * result
    return jnp.clip(result, min=-reach, max=reach).astype(kind)


def setup_inputs(seed: int = 0) -> dict:
    streams_of = jax.random.split(jax.random.key(seed), 8)
    return {
        "tile": centred(streams_of[0], (ROWS, D), 1.0, 6.0, ((0, 512),)),
        "cotangent": centred(streams_of[1], (ROWS, D), 1.0, 6.0, ((0, 512),)),
        "combine": jnp.clip(0.05 + 0.55 * jax.random.uniform(streams_of[2], (ROWS,), jnp.float32) ** block_scale(streams_of[2], (ROWS,), ((0, 512),), -0.2, 0.2), 0.05, 0.6),
        "valid": draw_valid(jax.random.fold_in(streams_of[7], 71), 0),
        "w_gate": centred(streams_of[4], (D, FF), D ** -0.5, 0.125, ((0, 16),)),
        "w_up": centred(streams_of[5], (D, FF), D ** -0.5, 0.125, ((0, 16),)),
        "w_down": centred(streams_of[6], (FF, D), FF ** -0.5, 0.21875, ((1, 16),)),
    }


def reference(tile, cotangent, combine, valid, w_gate, w_up, w_down):
    positions = jnp.arange(ROWS, dtype=jnp.int32)
    limits = jnp.repeat(valid, CAP)
    keep = (positions % CAP < limits).astype(jnp.float32)[:, None]
    gate = jnp.dot(tile, w_gate, preferred_element_type=jnp.float32)
    up = jnp.dot(tile, w_up, preferred_element_type=jnp.float32)
    hidden = (jax.nn.silu(gate) * up).astype(jnp.bfloat16)
    expert_out = jnp.dot(hidden, w_down, preferred_element_type=jnp.float32)
    weight = keep * combine[:, None]
    output = (weight * expert_out).astype(jnp.bfloat16)
    width_scale = 1.0 / jnp.sqrt(jnp.float32(D))
    combine_grad = keep[:, 0] * lax.optimization_barrier(jnp.sum(cotangent.astype(jnp.float32) * expert_out, axis=1)) * width_scale
    dy = (weight * cotangent.astype(jnp.float32)).astype(jnp.bfloat16)
    dhidden = jnp.dot(dy, w_down.T, preferred_element_type=jnp.float32)
    sig = jax.nn.sigmoid(gate)
    dgate = (dhidden * up * sig * (1.0 + gate * (1.0 - sig))).astype(jnp.bfloat16)
    dup = (dhidden * gate * sig).astype(jnp.bfloat16)
    tile_grad = (jnp.dot(dgate, w_gate.T, preferred_element_type=jnp.float32) + jnp.dot(dup, w_up.T, preferred_element_type=jnp.float32)).astype(jnp.bfloat16)
    factor = 1.0 / jnp.sqrt(jnp.float32(ROWS))
    grad_gate = jnp.dot(tile.T, dgate, preferred_element_type=jnp.float32) * factor
    grad_up = jnp.dot(tile.T, dup, preferred_element_type=jnp.float32) * factor
    grad_down = jnp.dot(hidden.T, dy, preferred_element_type=jnp.float32) * factor
    return (output, tile_grad, combine_grad, grad_gate, grad_up, grad_down)
```

```python
import functools
import math

import jax
import jax.numpy as jnp
from jax import lax
from jax.experimental import pallas as pl
from jax.experimental.pallas import tpu as pltpu
from jax.sharding import PartitionSpec as P

MESH = pl.DeviceIdType.MESH
ROWS = 128
D = 2048
FF = 768
NZ = 16
CHUNKS = 3
PART = 64
BLOCK = 3 * PART
LANES = 128
HALF = BLOCK // 2
F32 = jnp.float32
BF16 = jnp.bfloat16


def dot_nt(left, right):
    return lax.dot_general(left, right, (((1,), (1,)), ((), ())), preferred_element_type=F32)


def dot_nn(left, right):
    return jnp.dot(left, right, preferred_element_type=F32)


def kernel(
    tile, cot, comb, valid, wg, wu, wd,
    out_o, tg_o, cg_o, gr_o,
    wf, wbuf, gbuf, rsib, xbuf, dybuf, weight, hbuf, dgubuf, hT, dguT,
    own, psnd, prcv,
    bsnd, brel, bfin, bacc, asnd, arel, afin, zf, zsnd, zrcv,
    send_sems, recv_sems,
):
    dp = lax.axis_index("dp")
    fs = lax.axis_index("fsdp")
    z, c = dp // 2, dp % 2
    y, x = fs // 4, fs % 4
    h, zh = z % 2, z // 2
    a = x + c * (y - x)
    b = y + c * (x - y)

    def at_ab(aa, bb):
        return (dp, (bb + c * (aa - bb)) * 4 + aa + c * (bb - aa))

    a_r, a_l = at_ab((a + 1) % 4, b), at_ab((a + 3) % 4, b)
    b_r, b_l = at_ab(a, (b + 1) % 4), at_ab(a, (b + 3) % 4)
    sib = (z * 2 + 1 - c, fs)
    pz = (z + 1 - 2 * ((z + c) % 2) + NZ) % NZ
    pair = (pz * 2 + c, fs)
    peers = [((((zh + j) % 8) * 2 + h) * 2 + c, fs) for j in range(1, 8)]

    barrier = pltpu.get_barrier_semaphore()
    everyone = [a_r, a_l, b_r, b_l, sib, pair] + peers
    for dev in everyone:
        pl.semaphore_signal(barrier, inc=1, device_id=dev, device_id_type=MESH)

    copies = {}

    def send(name, src, dst, dev):
        n = len(copies)
        copy = pltpu.make_async_remote_copy(
            src_ref=src, dst_ref=dst, send_sem=send_sems.at[n], recv_sem=recv_sems.at[n],
            device_id=dev, device_id_type=MESH,
        )
        copies[name] = copy
        copy.start()

    def arrived(*name):
        copies[name].wait_recv()

    wf[0] = wg[...].astype(F32).T
    wf[1] = wu[...].astype(F32).T
    wf[2] = wd[...].astype(F32)
    for k in range(CHUNKS):
        for m in range(3):
            rows = [
                wf[m, pl.ds(pl.multiple_of(((t * 2 + h) * 2 + c) * 24 + k * 8, 8), 8), :]
                for t in range(8)
            ]
            wbuf[k, c, b, a, m * PART:(m + 1) * PART, :] = jnp.concatenate(rows, 0).astype(BF16)

    kept = lax.broadcasted_iota(jnp.int32, (ROWS, LANES), 1) < valid[0]
    spread = jnp.broadcast_to(comb[...], (ROWS, LANES))
    weight[0] = jnp.where(kept, spread, 0.0).T
    weight[1] = jnp.where(kept, jnp.ones_like(spread), 0.0).T
    xbuf[0:ROWS, :] = tile[...]
    for s in range(16):
        cols = slice(s * LANES, (s + 1) * LANES)
        dybuf[0:ROWS, cols] = (weight[0] * cot[:, cols].astype(F32)).astype(BF16)

    pl.semaphore_wait(barrier, len(everyone))

    def a_start(k):
        block = wbuf.at[k, c, b, a]
        send(("aR", k), block, block, a_r)
        send(("aL", k), block, block, a_l)

    def a_fwd(k):
        arrived("aR", k)
        block = wbuf.at[k, c, b, (a + 3) % 4, 0:HALF]
        send(("aRR", k), block, block, a_r)
        arrived("aL", k)
        block = wbuf.at[k, c, b, (a + 1) % 4, HALF:BLOCK]
        send(("aLL", k), block, block, a_l)

    def b_start(k):
        arrived("aRR", k)
        arrived("aLL", k)
        slab = wbuf.at[k, c, b]
        send(("bR", k), slab, slab, b_r)
        send(("bL", k), slab, slab, b_l)
        send(("sib0", k), slab, slab, sib)

    def b_fwd(k):
        arrived("bR", k)
        slab = wbuf.at[k, c, (b + 3) % 4]
        send(("bRR", k), slab.at[0:2], slab.at[0:2], b_r)
        send(("sib1", k), slab, slab, sib)
        arrived("bL", k)
        slab = wbuf.at[k, c, (b + 1) % 4]
        send(("bLL", k), slab.at[2:4], slab.at[2:4], b_l)
        send(("sib2", k), slab, slab, sib)

    def b_done(k):
        arrived("bRR", k)
        arrived("bLL", k)
        slab = wbuf.at[k, c, (b + 2) % 4]
        send(("sib3", k), slab, slab, sib)

    def sib_wait(k):
        for i in range(4):
            arrived("sib%d" % i, k)

    def piece(k, m, p, yy, xx):
        at = (k, p, yy, xx) if p == 0 else (k, p, xx, yy)
        return wbuf[at + (slice(m * PART, (m + 1) * PART), slice(None))]

    def wrows(k, m, ys):
        return jnp.concatenate(
            [
                jnp.concatenate([piece(k, m, p, yy, xx) for yy in ys for xx in range(4)], 1)
                for p in range(2)
            ],
            0,
        )

    def hidden_part(k):
        every = range(4)
        w_gu = jnp.concatenate([wrows(k, 0, every), wrows(k, 1, every)], 0)
        gu = dot_nt(xbuf[...], w_gu)
        dh = dot_nt(dybuf[...], wrows(k, 2, every))
        gate, up = gu[:, 0:128], gu[:, 128:256]
        sig = jax.nn.sigmoid(gate)
        hidden = gate * sig * up
        dgate = dh * up * sig * (1.0 + gate * (1.0 - sig))
        dup = dh * gate * sig
        hbuf[:, k * 128:(k + 1) * 128] = hidden.astype(BF16)
        dgubuf[:, k * 256:k * 256 + 128] = dgate.astype(BF16)
        dgubuf[:, k * 256 + 128:(k + 1) * 256] = dup.astype(BF16)
        hT[...] = hidden.T.astype(BF16)
        dguT[0:128, :] = dgate.T.astype(BF16)
        dguT[128:256, :] = dup.T.astype(BF16)

    def grads(k):
        def body(yy, _):
            cols = pl.ds(pl.multiple_of(yy * 512, 512), 512)
            g_gu = dot_nn(dguT[...], xbuf[:, cols])
            g_d = dot_nn(hT[...], dybuf[:, cols])
            for m in range(3):
                for p in range(2):
                    for xx in range(4):
                        at = (k, p, yy, xx) if p == 0 else (k, p, xx, yy)
                        base = p * PART + (m * 128 if m < 2 else 0)
                        g = (g_gu if m < 2 else g_d)[base:base + PART, xx * 128:(xx + 1) * 128]
                        gbuf[at + (slice(m * PART, (m + 1) * PART), slice(None))] = g.astype(BF16)
            return 0

        lax.fori_loop(0, 4, body, 0)
        for i, off in enumerate((2, 1, 3, 0)):
            bb = (a + off) % 4
            send(("gs%d" % i, k), gbuf.at[k, 1 - c, bb], rsib.at[k, bb], sib)

    def project(which):
        def body(yy, _):
            cols = pl.ds(pl.multiple_of(yy * 512, 512), 512)
            if which == 0:
                w = jnp.concatenate([wrows(k, 2, [yy]) for k in range(CHUNKS)], 0)
                res = dot_nn(hbuf[...], w)
            else:
                w = jnp.concatenate(
                    [wrows(k, m, [yy]) for k in range(CHUNKS) for m in range(2)], 0
                )
                res = dot_nn(dgubuf[...], w)
            own[which, :, cols] = res[0:ROWS]
            psnd[which, :, cols] = res[ROWS:2 * ROWS].astype(BF16)
            return 0

        lax.fori_loop(0, 4, body, 0)
        send(("p%d" % which,), psnd.at[which], prcv.at[which], pair)

    def gsum(k, bb, lo, hi):
        return gbuf[k, c, bb, lo:hi].astype(F32) + rsib[k, bb, lo:hi].astype(F32)

    def rb_start(k):
        arrived("gs0", k)
        bsnd[k, 0] = gsum(k, (b + 2) % 4, 0, 4).astype(BF16)
        send(("rbRR", k), bsnd.at[k, 0, 0:2], brel.at[k, 0], b_r)
        send(("rbLL", k), bsnd.at[k, 0, 2:4], brel.at[k, 1], b_l)
        arrived("gs1", k)
        bsnd[k, 1, 2:4] = gsum(k, (b + 1) % 4, 2, 4).astype(BF16)
        send(("rbR0", k), bsnd.at[k, 1, 2:4], bfin.at[k, 0, 2:4], b_r)
        arrived("gs2", k)
        bsnd[k, 2, 0:2] = gsum(k, (b + 3) % 4, 0, 2).astype(BF16)
        send(("rbL0", k), bsnd.at[k, 2, 0:2], bfin.at[k, 1, 0:2], b_l)

    def rb_relay(k):
        arrived("rbRR", k)
        bsnd[k, 1, 0:2] = (gsum(k, (b + 1) % 4, 0, 2) + brel[k, 0].astype(F32)).astype(BF16)
        send(("rbR1", k), bsnd.at[k, 1, 0:2], bfin.at[k, 0, 0:2], b_r)
        arrived("rbLL", k)
        bsnd[k, 2, 2:4] = (gsum(k, (b + 3) % 4, 2, 4) + brel[k, 1].astype(F32)).astype(BF16)
        send(("rbL1", k), bsnd.at[k, 2, 2:4], bfin.at[k, 1, 2:4], b_l)

    def rb_final(k):
        arrived("gs3", k)
        for name in ("rbR0", "rbL0", "rbR1", "rbL1"):
            arrived(name, k)
        bacc[k] = gsum(k, b, 0, 4) + bfin[k, 0].astype(F32) + bfin[k, 1].astype(F32)

    def ra_start(k):
        a2, ar, al = (a + 2) % 4, (a + 1) % 4, (a + 3) % 4
        asnd[k, 0] = bacc[k, a2].astype(BF16)
        send(("raRR", k), asnd.at[k, 0, 0:HALF], arel.at[k, 0], a_r)
        send(("raLL", k), asnd.at[k, 0, HALF:BLOCK], arel.at[k, 1], a_l)
        asnd[k, 1, HALF:BLOCK] = bacc[k, ar, HALF:BLOCK].astype(BF16)
        send(("raR0", k), asnd.at[k, 1, HALF:BLOCK], afin.at[k, 0, HALF:BLOCK], a_r)
        asnd[k, 2, 0:HALF] = bacc[k, al, 0:HALF].astype(BF16)
        send(("raL0", k), asnd.at[k, 2, 0:HALF], afin.at[k, 1, 0:HALF], a_l)

    def ra_relay(k):
        ar, al = (a + 1) % 4, (a + 3) % 4
        arrived("raRR", k)
        asnd[k, 1, 0:HALF] = (bacc[k, ar, 0:HALF] + arel[k, 0].astype(F32)).astype(BF16)
        send(("raR1", k), asnd.at[k, 1, 0:HALF], afin.at[k, 0, 0:HALF], a_r)
        arrived("raLL", k)
        asnd[k, 2, HALF:BLOCK] = (bacc[k, al, HALF:BLOCK] + arel[k, 1].astype(F32)).astype(BF16)
        send(("raL1", k), asnd.at[k, 2, HALF:BLOCK], afin.at[k, 1, HALF:BLOCK], a_l)

    def ra_final(k):
        for name in ("raR0", "raL0", "raR1", "raL1"):
            arrived(name, k)
        blk = bacc[k, a] + afin[k, 0].astype(F32) + afin[k, 1].astype(F32)
        for t in range(8):
            rows = jnp.concatenate([blk[m * PART + t * 8:m * PART + t * 8 + 8] for m in range(3)], 0)
            zf[k, t] = rows
            zsnd[k, t] = jnp.concatenate([rows, jnp.zeros((8, LANES), F32)], 0).astype(BF16)
        for j in range(1, 8):
            send(("z%d" % j, k), zsnd.at[k, (zh + j) % 8], zrcv.at[k, j - 1], peers[j - 1])

    def z_final(k):
        total = zf[k, zh]
        for j in range(1, 8):
            arrived("z%d" % j, k)
            total = total + zrcv[k, j - 1].astype(F32)[0:24]
        total = total * (1.0 / 256.0)
        for m in range(3):
            gr_o[m, k * 8:(k + 1) * 8, :] = total[m * 8:(m + 1) * 8]

    for k in range(CHUNKS):
        a_start(k)
    send(("tile",), xbuf.at[0:ROWS], xbuf.at[ROWS:2 * ROWS], pair)
    send(("dy",), dybuf.at[0:ROWS], dybuf.at[ROWS:2 * ROWS], pair)
    for k in range(CHUNKS):
        a_fwd(k)
    b_start(0)
    b_start(1)
    b_fwd(0)
    b_start(2)
    b_fwd(1)
    b_done(0)
    sib_wait(0)
    arrived("tile")
    arrived("dy")
    hidden_part(0)
    b_fwd(2)
    b_done(1)
    grads(0)
    sib_wait(1)
    hidden_part(1)
    b_done(2)
    grads(1)
    rb_start(0)
    sib_wait(2)
    hidden_part(2)
    grads(2)
    rb_relay(0)
    rb_start(1)
    project(0)
    rb_final(0)
    ra_start(0)
    rb_relay(1)
    rb_start(2)
    project(1)
    ra_relay(0)
    rb_final(1)
    ra_start(1)
    rb_relay(2)
    ra_final(0)
    ra_relay(1)
    rb_final(2)
    ra_start(2)
    ra_final(1)
    ra_relay(2)
    ra_final(2)

    arrived("p0")
    dots = jnp.zeros((ROWS, LANES), F32)
    for s in range(16):
        cols = slice(s * LANES, (s + 1) * LANES)
        full = own[0, :, cols] + prcv[0, :, cols].astype(F32)
        out_o[:, cols] = (weight[0] * full).astype(BF16)
        dots = dots + cot[:, cols].astype(F32) * full
    total = jnp.broadcast_to(jnp.sum(dots, axis=1, keepdims=True), (ROWS, LANES))
    total = total * weight[1] * (1.0 / math.sqrt(D))
    cg_o[...] = total.T[0:1, :]
    arrived("p1")
    for s in range(16):
        cols = slice(s * LANES, (s + 1) * LANES)
        tg_o[:, cols] = (own[1, :, cols] + prcv[1, :, cols].astype(F32)).astype(BF16)
    for k in range(CHUNKS):
        z_final(k)
    for copy in copies.values():
        copy.wait_send()


N_COPIES = 36 + 23 * CHUNKS + 4


def on_device(tile, cotangent, combine, valid, w_gate, w_up, w_down):
    vmem = pl.BlockSpec(memory_space=pltpu.VMEM)
    smem = pl.BlockSpec(memory_space=pltpu.SMEM)
    k = CHUNKS
    out, tg, cg, gr = pl.pallas_call(
        kernel,
        out_shape=(
            jax.ShapeDtypeStruct((ROWS, D), BF16),
            jax.ShapeDtypeStruct((ROWS, D), BF16),
            jax.ShapeDtypeStruct((1, ROWS), F32),
            jax.ShapeDtypeStruct((3, 24, LANES), F32),
        ),
        in_specs=[vmem, vmem, vmem, smem, vmem, vmem, vmem],
        out_specs=(vmem, vmem, vmem, vmem),
        scratch_shapes=[
            pltpu.VMEM((3, FF, LANES), F32),
            pltpu.VMEM((k, 2, 4, 4, BLOCK, LANES), BF16),
            pltpu.VMEM((k, 2, 4, 4, BLOCK, LANES), BF16),
            pltpu.VMEM((k, 4, 4, BLOCK, LANES), BF16),
            pltpu.VMEM((2 * ROWS, D), BF16),
            pltpu.VMEM((2 * ROWS, D), BF16),
            pltpu.VMEM((2, ROWS, LANES), F32),
            pltpu.VMEM((2 * ROWS, k * 128), BF16),
            pltpu.VMEM((2 * ROWS, k * 256), BF16),
            pltpu.VMEM((128, 2 * ROWS), BF16),
            pltpu.VMEM((256, 2 * ROWS), BF16),
            pltpu.VMEM((2, ROWS, D), F32),
            pltpu.VMEM((2, ROWS, D), BF16),
            pltpu.VMEM((2, ROWS, D), BF16),
            pltpu.VMEM((k, 3, 4, BLOCK, LANES), BF16),
            pltpu.VMEM((k, 2, 2, BLOCK, LANES), BF16),
            pltpu.VMEM((k, 2, 4, BLOCK, LANES), BF16),
            pltpu.VMEM((k, 4, BLOCK, LANES), F32),
            pltpu.VMEM((k, 3, BLOCK, LANES), BF16),
            pltpu.VMEM((k, 2, HALF, LANES), BF16),
            pltpu.VMEM((k, 2, BLOCK, LANES), BF16),
            pltpu.VMEM((k, 8, 24, LANES), F32),
            pltpu.VMEM((k, 8, 32, LANES), BF16),
            pltpu.VMEM((k, 7, 32, LANES), BF16),
            pltpu.SemaphoreType.DMA((N_COPIES,)),
            pltpu.SemaphoreType.DMA((N_COPIES,)),
        ],
        compiler_params=pltpu.CompilerParams(
            collective_id=0, has_side_effects=True, vmem_limit_bytes=52 * 1024 * 1024
        ),
        cost_estimate=pl.CostEstimate(
            flops=18 * ROWS * D * FF, bytes_accessed=4 * 1024 * 1024, transcendentals=ROWS * FF
        ),
    )(tile, cotangent, combine.reshape(1, ROWS), valid, w_gate, w_up, w_down)
    return (out, tg, cg.reshape(ROWS), gr[0].T, gr[1].T, gr[2])


def solution(mesh):
    in_specs = (
        P(("dp", "fsdp"), None),
        P(("dp", "fsdp"), None),
        P(("dp", "fsdp")),
        P(("dp", "fsdp")),
        P("fsdp", None),
        P("fsdp", None),
        P(None, "fsdp"),
    )
    out_specs = (
        P(("dp", "fsdp"), None),
        P(("dp", "fsdp"), None),
        P(("dp", "fsdp")),
        P("fsdp", "dp"),
        P("fsdp", "dp"),
        P("dp", "fsdp"),
    )
    return jax.shard_map(
        on_device, mesh=mesh, in_specs=in_specs, out_specs=out_specs, check_vma=False
    )
```

```python
import functools
import math

import jax
import jax.numpy as jnp
from jax import lax
from jax.experimental import pallas as pl
from jax.experimental.pallas import tpu as pltpu
from jax.sharding import PartitionSpec as P

MESH = pl.DeviceIdType.MESH
ROWS = 128
D = 2048
FF = 768
NZ = 16
N_RELAYED = 0
CHUNKS = 3
PART = 64
BLOCK = 3 * PART
LANES = 128
F32 = jnp.float32
BF16 = jnp.bfloat16


def dot_nt(left, right):
    return lax.dot_general(left, right, (((1,), (1,)), ((), ())), preferred_element_type=F32)


def dot_nn(left, right):
    return jnp.dot(left, right, preferred_element_type=F32)


VMEM_BYTES = 60 * 1024 * 1024


def hand_over(*refs):
    ins, outs, held, sems = refs[:4], refs[4:10], refs[10:14], refs[14]
    loads = [
        pltpu.make_async_copy(src, dst, sems.at[n]) for n, (src, dst) in enumerate(zip(ins, held))
    ]
    parts = [(0, held[0]), (1, held[1]), (2, held[2])] + [(3, held[3].at[m]) for m in range(3)]
    stores = [
        pltpu.make_async_copy(src, dst, sems.at[4 + n])
        for n, ((_, src), dst) in enumerate(zip(parts, outs))
    ]
    for load in loads:
        load.start()
    for n, load in enumerate(loads):
        load.wait()
        for (of, _), store in zip(parts, stores):
            if of == n:
                store.start()
    for store in stores:
        store.wait()


def kernel(
    tile, cot, comb, valid, wg, wu, wd,
    out_o, tg_o, cg_o, gr_o,
    wg_v, wu_v, wd_v, cot_v, comb_v, valid_s,
    wbuf, gbuf, rsib, xbuf, dybuf, weight, hbuf, dgubuf, hT, dguT,
    own, psnd, prcv, fin,
    bsnd, brel, bfin, bacc, asnd, afin, zf, zsnd, zrcv,
    load_sems, store_sems, send_sems, recv_sems,
):
    dp = lax.axis_index("dp")
    fs = lax.axis_index("fsdp")
    z, c = dp // 2, dp % 2
    y, x = fs // 4, fs % 4
    h, zh = z % 2, z // 2
    a = x + c * (y - x)
    b = y + c * (x - y)

    def at_ab(aa, bb):
        return (dp, (bb + c * (aa - bb)) * 4 + aa + c * (bb - aa))

    a_to = [at_ab((a + o) % 4, b) for o in range(4)]
    b_to = [at_ab(a, (b + o) % 4) for o in range(4)]
    sib = (z * 2 + 1 - c, fs)
    pz = (z + 1 - 2 * ((z + c) % 2) + NZ) % NZ
    pair = (pz * 2 + c, fs)
    peers = [((((zh + j) % 8) * 2 + h) * 2 + c, fs) for j in range(1, 8)]

    loads = [
        pltpu.make_async_copy(src, dst, load_sems.at[n])
        for n, (src, dst) in enumerate(
            [
                (wg, wg_v), (wu, wu_v), (wd, wd_v), (comb, comb_v),
                (tile, xbuf.at[0:ROWS]), (cot, cot_v), (valid, valid_s),
            ]
        )
    ]
    for load in loads[0:3]:
        load.start()
    barrier = pltpu.get_barrier_semaphore()
    everyone = a_to[1:] + b_to[1:] + [sib, pair] + peers
    for dev in everyone:
        pl.semaphore_signal(barrier, inc=1, device_id=dev, device_id_type=MESH)
    for load in loads[3:]:
        load.start()

    copies, gone = {}, set()

    def send(name, src, dst, dev):
        n = len(copies)
        copy = pltpu.make_async_remote_copy(
            src_ref=src, dst_ref=dst, send_sem=send_sems.at[n], recv_sem=recv_sems.at[n],
            device_id=dev, device_id_type=MESH,
        )
        copies[name] = copy
        copy.start()

    def arrived(*name):
        copies[name].wait_recv()

    def sent(*names):
        for name in names:
            copies[name].wait_send()
            gone.add(name)

    row = lax.broadcasted_iota(jnp.int32, (CHUNKS * PART, LANES), 0)
    lane = lax.broadcasted_iota(jnp.int32, (CHUNKS * PART, LANES), 1)
    unit = (((row % PART) // 8 * 2 + h) * 2 + c) * 24 + row // PART * 8 + row % 8 - lane
    pick = jnp.concatenate(
        [jnp.where(unit == n * LANES, 1.0, 0.0).astype(BF16) for n in range(FF // LANES)], 1
    )
    for m in range(3):
        loads[m].wait()
        rows = dot_nt(pick, (wg_v, wu_v)[m][...]) if m < 2 else dot_nn(pick, wd_v[...])
        for k in range(CHUNKS):
            wbuf[k, c, b, a, m * PART:(m + 1) * PART, :] = rows[k * PART:(k + 1) * PART].astype(BF16)

    pl.semaphore_wait(barrier, len(everyone))

    def own_start(k):
        block = wbuf.at[k, c, b, a]
        for o in (2, 1, 3):
            send(("a", o, k), block, block, a_to[o])
        for o in (1, 3):
            send(("b", o, 0, k), block, block, b_to[o])

    def slab_start(k):
        for o in (3, 1, 2):
            arrived("a", (4 - o) % 4, k)
            block = wbuf.at[k, c, b, (a + o) % 4]
            for to in (1, 3):
                send(("b", to, o, k), block, block, b_to[to])
        slab = wbuf.at[k, c, b]
        send(("sib0", k), slab, slab, sib)

    def forward(k, to, o):
        arrived("b", to, o, k)
        block = wbuf.at[k, c, (b + 4 - to) % 4, (a + o) % 4]
        send(("f", to, o, k), block, block, b_to[to])

    def slabs_in(k):
        for to in (1, 3):
            for o in ((1, 3) if to == 1 else (0, 2)):
                arrived("b", to, o, k)
            slab = wbuf.at[k, c, (b + 4 - to) % 4]
            send(("sib%d" % to, k), slab, slab, sib)

    def last_slab_in(k):
        for to, o in ((1, 0), (1, 2), (3, 1), (3, 3)):
            arrived("f", to, o, k)
        slab = wbuf.at[k, c, (b + 2) % 4]
        send(("sib2", k), slab, slab, sib)

    def sib_wait(k):
        for i in range(4):
            arrived("sib%d" % i, k)

    def piece(k, m, p, yy, xx):
        at = (k, p, yy, xx) if p == 0 else (k, p, xx, yy)
        return wbuf[at + (slice(m * PART, (m + 1) * PART), slice(None))]

    def wrows(k, m, ys):
        return jnp.concatenate(
            [
                jnp.concatenate([piece(k, m, p, yy, xx) for yy in ys for xx in range(4)], 1)
                for p in range(2)
            ],
            0,
        )

    def hidden_part(k):
        every = range(4)
        w_gu = jnp.concatenate([wrows(k, 0, every), wrows(k, 1, every)], 0)
        gu = dot_nt(xbuf[...], w_gu)
        dh = dot_nt(dybuf[...], wrows(k, 2, every))
        gate, up = gu[:, 0:128], gu[:, 128:256]
        sig = jax.nn.sigmoid(gate)
        hidden = gate * sig * up
        dgate = dh * up * sig * (1.0 + gate * (1.0 - sig))
        dup = dh * gate * sig
        hbuf[:, k * 128:(k + 1) * 128] = hidden.astype(BF16)
        dgubuf[:, k * 256:k * 256 + 128] = dgate.astype(BF16)
        dgubuf[:, k * 256 + 128:(k + 1) * 256] = dup.astype(BF16)
        hT[...] = hidden.T.astype(BF16)
        dguT[0:128, :] = dgate.T.astype(BF16)
        dguT[128:256, :] = dup.T.astype(BF16)

    def grads(k):
        def body(yy, _):
            cols = pl.ds(pl.multiple_of(yy * 512, 512), 512)
            g_gu = dot_nn(dguT[...], xbuf[:, cols])
            g_d = dot_nn(hT[...], dybuf[:, cols])
            for m in range(3):
                for p in range(2):
                    for xx in range(4):
                        at = (k, p, yy, xx) if p == 0 else (k, p, xx, yy)
                        base = p * PART + (m * 128 if m < 2 else 0)
                        g = (g_gu if m < 2 else g_d)[base:base + PART, xx * 128:(xx + 1) * 128]
                        gbuf[at + (slice(m * PART, (m + 1) * PART), slice(None))] = g.astype(BF16)
            return 0

        lax.fori_loop(0, 4, body, 0)

    def grads_send(k):
        for i, off in enumerate((2, 1, 3, 0)):
            bb = (a + off) % 4
            send(("gs%d" % i, k), gbuf.at[k, 1 - c, bb], rsib.at[k, bb], sib)

    def project(which):
        def body(yy, _):
            cols = pl.ds(pl.multiple_of(yy * 512, 512), 512)
            if which == 0:
                w = jnp.concatenate([wrows(k, 2, [yy]) for k in range(CHUNKS)], 0)
                res = dot_nn(hbuf[...], w)
            else:
                w = jnp.concatenate(
                    [wrows(k, m, [yy]) for k in range(CHUNKS) for m in range(2)], 0
                )
                res = dot_nn(dgubuf[...], w)
            own[which, :, cols] = res[0:ROWS]
            psnd[which, :, cols] = res[ROWS:2 * ROWS].astype(BF16)
            return 0

        lax.fori_loop(0, 4, body, 0)

    def pair_send(which):
        send(("p%d" % which,), psnd.at[which], prcv.at[which], pair)

    def gsum(k, bb, i):
        return gbuf[k, c, bb, i].astype(F32) + rsib[k, bb, i].astype(F32)

    def rb_sum(k, o, lo, hi, more=None):
        def body(i, _):
            total = gsum(k, (b + o) % 4, i)
            if more is not None:
                total = total + brel[k, more, i - lo].astype(F32)
            bsnd[k, o - 1, i] = total.astype(BF16)
            return 0

        lax.fori_loop(lo, hi, body, 0)

    def rb_send(k, o, lo, hi):
        part = slice(lo, hi)
        send(("rb", o, lo, k), bsnd.at[k, o - 1, part], bfin.at[k, o - 1, part], b_to[o])

    def rb_start(k):
        arrived("gs0", k)
        rb_sum(k, 2, 0, 4)
        if k < N_RELAYED:
            send(("rr", 1, k), bsnd.at[k, 1, 0:2], brel.at[k, 0], b_to[1])
            send(("rr", 3, k), bsnd.at[k, 1, 2:4], brel.at[k, 1], b_to[3])
        else:
            rb_send(k, 2, 0, 4)
        for i, o in ((1, 1), (2, 3)):
            arrived("gs%d" % i, k)
            lo, hi = ((2, 4) if o == 1 else (0, 2)) if k < N_RELAYED else (0, 4)
            rb_sum(k, o, lo, hi)
            rb_send(k, o, lo, hi)

    def rb_sent(k):
        if k < N_RELAYED:
            sent(("rr", 1, k), ("rr", 3, k), ("rb", 1, 2, k), ("rb", 3, 0, k))
        else:
            sent(*((("rb", o, 0, k)) for o in (1, 2, 3)))

    def rb_relay(k):
        for n, o in enumerate((1, 3)):
            arrived("rr", o, k)
            lo, hi = (0, 2) if o == 1 else (2, 4)
            rb_sum(k, o, lo, hi, n)
            rb_send(k, o, lo, hi)

    def ra_start(k):
        arrived("gs3", k)
        if k < N_RELAYED:
            waits, terms = [(1, 0), (1, 2), (3, 0), (3, 2)], (1, 3)
        else:
            waits, terms = [(1, 0), (3, 0), (2, 0)], (1, 3, 2)
        for o, lo in waits:
            arrived("rb", o, lo, k)
        for o in (2, 1, 3, 0):
            i = (a + o) % 4
            total = gsum(k, b, i)
            for t in terms:
                total = total + bfin[k, t - 1, i].astype(F32)
            if o:
                asnd[k, o - 1] = total.astype(BF16)
                send(("ra", o, k), asnd.at[k, o - 1], afin.at[k, o - 1], a_to[o])
            else:
                bacc[k] = total

    def ra_final(k):
        blk = bacc[k]
        for o in (1, 3, 2):
            arrived("ra", o, k)
            blk = blk + afin[k, o - 1].astype(F32)
        for t in range(8):
            rows = jnp.concatenate([blk[m * PART + t * 8:m * PART + t * 8 + 8] for m in range(3)], 0)
            zf[k, t] = rows
            zsnd[k, t] = jnp.concatenate([rows, jnp.zeros((8, LANES), F32)], 0).astype(BF16)
        for j in (4, 3, 5, 2, 6, 1, 7):
            send(("z%d" % j, k), zsnd.at[k, (zh + j) % 8], zrcv.at[k, j - 1], peers[j - 1])

    def z_final(k):
        total = zf[k, zh]
        for j in range(1, 8):
            arrived("z%d" % j, k)
            total = total + zrcv[k, j - 1].astype(F32)[0:24]
        total = total * (1.0 / 256.0)
        for m in range(3):
            gr_o[m, k * 8:(k + 1) * 8, :] = total[m * 8:(m + 1) * 8]

    def tile_send():
        send(("tile",), tile, xbuf.at[ROWS:2 * ROWS], pair)

    def dy_send():
        loads[3].wait()
        loads[6].wait()
        kept = lax.broadcasted_iota(jnp.int32, (ROWS, LANES), 1) < valid_s[0]
        spread = jnp.broadcast_to(comb_v[...], (ROWS, LANES))
        weight[0] = jnp.where(kept, spread, 0.0).T
        weight[1] = jnp.where(kept, jnp.ones_like(spread), 0.0).T
        loads[5].wait()
        for s in range(16):
            cols = slice(s * LANES, (s + 1) * LANES)
            dybuf[0:ROWS, cols] = (weight[0] * cot_v[:, cols].astype(F32)).astype(BF16)
        send(("dy",), dybuf.at[0:ROWS], dybuf.at[ROWS:2 * ROWS], pair)

    def rows_wait():
        loads[4].wait()
        arrived("tile")
        arrived("dy")

    stores = [
        pltpu.make_async_copy(fin.at[n], ref, store_sems.at[n]) for n, ref in enumerate((out_o, tg_o))
    ]

    def output_final():
        arrived("p0")

        def body(s, dots):
            cols = pl.ds(pl.multiple_of(s * LANES, LANES), LANES)
            full = own[0, :, cols] + prcv[0, :, cols].astype(F32)
            fin[0, :, cols] = (weight[0] * full).astype(BF16)
            return dots + cot_v[:, cols].astype(F32) * full

        dots = lax.fori_loop(0, 16, body, jnp.zeros((ROWS, LANES), F32))
        stores[0].start()
        total = jnp.broadcast_to(jnp.sum(dots, axis=1, keepdims=True), (ROWS, LANES))
        total = total * weight[1] * (1.0 / math.sqrt(D))
        cg_o[...] = total.T[0:1, :]

    def tile_grad_final():
        arrived("p1")

        def body(s, _):
            cols = pl.ds(pl.multiple_of(s * LANES, LANES), LANES)
            fin[1, :, cols] = (own[1, :, cols] + prcv[1, :, cols].astype(F32)).astype(BF16)
            return 0

        lax.fori_loop(0, 16, body, 0)
        stores[1].start()

    tile_send()
    own_start(0)
    dy_send()
    own_start(1)
    slab_start(0)
    forward(0, 1, 0)
    own_start(2)
    slab_start(1)
    forward(0, 3, 1)
    forward(0, 3, 3)
    forward(0, 1, 2)
    slabs_in(0)
    forward(1, 1, 0)
    slab_start(2)
    last_slab_in(0)
    forward(1, 3, 1)
    forward(1, 3, 3)
    forward(1, 1, 2)
    slabs_in(1)
    forward(2, 1, 0)
    rows_wait()
    sib_wait(0)
    hidden_part(0)
    forward(2, 3, 1)
    forward(2, 3, 3)
    forward(2, 1, 2)
    slabs_in(2)
    last_slab_in(1)
    grads(0)
    grads_send(0)
    sib_wait(1)
    hidden_part(1)
    last_slab_in(2)
    rb_start(0)
    grads(1)
    grads_send(1)
    sib_wait(2)
    hidden_part(2)
    grads(2)
    grads_send(2)
    rb_start(1)
    project(0)
    pair_send(0)
    rb_start(2)
    ra_start(0)
    project(1)
    pair_send(1)
    ra_start(1)
    ra_final(0)
    ra_start(2)
    output_final()
    ra_final(1)
    ra_final(2)
    tile_grad_final()
    for k in range(CHUNKS):
        z_final(k)
    for store in stores:
        store.wait()
    sent(*(name for name in copies if name not in gone))


N_COPIES = (19 + 4 + 6 + 7) * CHUNKS + 3 * N_RELAYED + 4


def on_device(tile, cotangent, combine, valid, w_gate, w_up, w_down):
    vmem = pl.BlockSpec(memory_space=pltpu.VMEM)
    hbm = pl.BlockSpec(memory_space=pltpu.HBM)
    k = CHUNKS
    out, tg, cg, gr = pl.pallas_call(
        kernel,
        out_shape=(
            jax.ShapeDtypeStruct((ROWS, D), BF16),
            jax.ShapeDtypeStruct((ROWS, D), BF16),
            jax.ShapeDtypeStruct((1, ROWS), F32),
            jax.ShapeDtypeStruct((3, 24, LANES), F32),
        ),
        in_specs=[hbm] * 7,
        out_specs=(hbm, hbm, vmem, vmem),
        scratch_shapes=[
            pltpu.VMEM((LANES, FF), BF16),
            pltpu.VMEM((LANES, FF), BF16),
            pltpu.VMEM((FF, LANES), BF16),
            pltpu.VMEM((ROWS, D), BF16),
            pltpu.VMEM((1, ROWS), F32),
            pltpu.SMEM((1,), jnp.int32),
            pltpu.VMEM((k, 2, 4, 4, BLOCK, LANES), BF16),
            pltpu.VMEM((k, 2, 4, 4, BLOCK, LANES), BF16),
            pltpu.VMEM((k, 4, 4, BLOCK, LANES), BF16),
            pltpu.VMEM((2 * ROWS, D), BF16),
            pltpu.VMEM((2 * ROWS, D), BF16),
            pltpu.VMEM((2, ROWS, LANES), F32),
            pltpu.VMEM((2 * ROWS, k * 128), BF16),
            pltpu.VMEM((2 * ROWS, k * 256), BF16),
            pltpu.VMEM((128, 2 * ROWS), BF16),
            pltpu.VMEM((256, 2 * ROWS), BF16),
            pltpu.VMEM((2, ROWS, D), F32),
            pltpu.VMEM((2, ROWS, D), BF16),
            pltpu.VMEM((2, ROWS, D), BF16),
            pltpu.VMEM((2, ROWS, D), BF16),
            pltpu.VMEM((k, 3, 4, BLOCK, LANES), BF16),
            pltpu.VMEM((k, 2, 2, BLOCK, LANES), BF16),
            pltpu.VMEM((k, 3, 4, BLOCK, LANES), BF16),
            pltpu.VMEM((k, BLOCK, LANES), F32),
            pltpu.VMEM((k, 3, BLOCK, LANES), BF16),
            pltpu.VMEM((k, 3, BLOCK, LANES), BF16),
            pltpu.VMEM((k, 8, 24, LANES), F32),
            pltpu.VMEM((k, 8, 32, LANES), BF16),
            pltpu.VMEM((k, 7, 32, LANES), BF16),
            pltpu.SemaphoreType.DMA((7,)),
            pltpu.SemaphoreType.DMA((2,)),
            pltpu.SemaphoreType.DMA((N_COPIES,)),
            pltpu.SemaphoreType.DMA((N_COPIES,)),
        ],
        compiler_params=pltpu.CompilerParams(
            collective_id=0, has_side_effects=True, vmem_limit_bytes=VMEM_BYTES
        ),
        cost_estimate=pl.CostEstimate(
            flops=18 * ROWS * D * FF, bytes_accessed=4 * 1024 * 1024, transcendentals=ROWS * FF
        ),
    )(tile, cotangent, combine.reshape(1, ROWS), valid, w_gate, w_up, w_down)
    grad = jax.ShapeDtypeStruct((24, LANES), F32)
    out, tg, cg, gg, gu, gd = pl.pallas_call(
        hand_over,
        out_shape=(
            jax.ShapeDtypeStruct((ROWS, D), BF16),
            jax.ShapeDtypeStruct((ROWS, D), BF16),
            jax.ShapeDtypeStruct((1, ROWS), F32),
            grad, grad, grad,
        ),
        in_specs=[hbm] * 4,
        out_specs=(hbm,) * 6,
        scratch_shapes=[
            pltpu.VMEM((ROWS, D), BF16),
            pltpu.VMEM((ROWS, D), BF16),
            pltpu.VMEM((1, ROWS), F32),
            pltpu.VMEM((3, 24, LANES), F32),
            pltpu.SemaphoreType.DMA((10,)),
        ],
        compiler_params=pltpu.CompilerParams(vmem_limit_bytes=VMEM_BYTES),
    )(out, tg, cg, gr)
    return (out, tg, cg.reshape(ROWS), gg.T, gu.T, gd)


def solution(mesh):
    in_specs = (
        P(("dp", "fsdp"), None),
        P(("dp", "fsdp"), None),
        P(("dp", "fsdp")),
        P(("dp", "fsdp")),
        P("fsdp", None),
        P("fsdp", None),
        P(None, "fsdp"),
    )
    out_specs = (
        P(("dp", "fsdp"), None),
        P(("dp", "fsdp"), None),
        P(("dp", "fsdp")),
        P("fsdp", "dp"),
        P("fsdp", "dp"),
        P("dp", "fsdp"),
    )
    return jax.shard_map(
        on_device, mesh=mesh, in_specs=in_specs, out_specs=out_specs, check_vma=False
    )
```

```python
import functools
import math

import jax
import jax.numpy as jnp
from jax import lax
from jax.experimental import pallas as pl
from jax.experimental.pallas import tpu as pltpu
from jax.sharding import PartitionSpec as P

MESH = pl.DeviceIdType.MESH
ROWS = 128
D = 2048
FF = 768
NZ = 16
N_RELAYED = 0
CHUNKS = 3
PART = 64
BLOCK = 3 * PART
LANES = 128
F32 = jnp.float32
BF16 = jnp.bfloat16


def dot_nt(left, right):
    return lax.dot_general(left, right, (((1,), (1,)), ((), ())), preferred_element_type=F32)


def dot_nn(left, right):
    return jnp.dot(left, right, preferred_element_type=F32)


VMEM_BYTES = 60 * 1024 * 1024


def hand_over(*refs):
    ins, outs, held, sems = refs[:4], refs[4:10], refs[10:14], refs[14]
    loads = [
        pltpu.make_async_copy(src, dst, sems.at[n]) for n, (src, dst) in enumerate(zip(ins, held))
    ]
    parts = [(0, held[0]), (1, held[1]), (2, held[2])] + [(3, held[3].at[m]) for m in range(3)]
    stores = [
        pltpu.make_async_copy(src, dst, sems.at[4 + n])
        for n, ((_, src), dst) in enumerate(zip(parts, outs))
    ]
    for load in loads:
        load.start()
    for n, load in enumerate(loads):
        load.wait()
        for (of, _), store in zip(parts, stores):
            if of == n:
                store.start()
    for store in stores:
        store.wait()


def kernel(
    tile, cot, comb, valid, wg, wu, wd,
    out_o, tg_o, cg_o, gr_o,
    wg_v, wu_v, wd_v, cot_v, comb_v, valid_s,
    wbuf, gbuf, rsib, xbuf, dybuf, weight, hbuf, dgubuf, hT, dguT,
    own, psnd, prcv, fin,
    bsnd, brel, bfin, bacc, asnd, afin, zf, zsnd, zrcv,
    load_sems, store_sems, send_sems, recv_sems,
):
    dp = lax.axis_index("dp")
    fs = lax.axis_index("fsdp")
    z, c = dp // 2, dp % 2
    y, x = fs // 4, fs % 4
    h, zh = z % 2, z // 2
    a = x + c * (y - x)
    b = y + c * (x - y)

    def at_ab(aa, bb):
        return (dp, (bb + c * (aa - bb)) * 4 + aa + c * (bb - aa))

    a_to = [at_ab((a + o) % 4, b) for o in range(4)]
    b_to = [at_ab(a, (b + o) % 4) for o in range(4)]
    sib = (z * 2 + 1 - c, fs)
    pz = (z + 1 - 2 * ((z + c) % 2) + NZ) % NZ
    pair = (pz * 2 + c, fs)
    peers = [((((zh + j) % 8) * 2 + h) * 2 + c, fs) for j in range(1, 8)]

    loads = [
        pltpu.make_async_copy(src, dst, load_sems.at[n])
        for n, (src, dst) in enumerate(
            [
                (wg, wg_v), (wu, wu_v), (wd, wd_v), (comb, comb_v),
                (tile, xbuf.at[0:ROWS]), (cot, cot_v), (valid, valid_s),
            ]
        )
    ]
    for load in loads[0:3]:
        load.start()
    barrier = pltpu.get_barrier_semaphore()
    everyone = a_to[1:] + b_to[1:] + [sib, pair] + peers
    for dev in everyone:
        pl.semaphore_signal(barrier, inc=1, device_id=dev, device_id_type=MESH)
    for load in loads[3:]:
        load.start()

    copies, gone = {}, set()

    def remote(n, src, dst, dev):
        return pltpu.make_async_remote_copy(
            src_ref=src, dst_ref=dst, send_sem=send_sems.at[n], recv_sem=recv_sems.at[n],
            device_id=dev, device_id_type=MESH,
        )

    def send(name, src, dst, dev):
        copies[name] = remote(len(copies), src, dst, dev)
        copies[name].start()

    def arrived(*name):
        copies[name].wait_recv()

    def sent(*names):
        for name in names:
            copies[name].wait_send()
            gone.add(name)

    row = lax.broadcasted_iota(jnp.int32, (CHUNKS * PART, LANES), 0)
    lane = lax.broadcasted_iota(jnp.int32, (CHUNKS * PART, LANES), 1)
    unit = (((row % PART) // 8 * 2 + h) * 2 + c) * 24 + row // PART * 8 + row % 8 - lane
    pick = jnp.concatenate(
        [jnp.where(unit == n * LANES, 1.0, 0.0).astype(BF16) for n in range(FF // LANES)], 1
    )
    for m in range(3):
        loads[m].wait()
        rows = dot_nt(pick, (wg_v, wu_v)[m][...]) if m < 2 else dot_nn(pick, wd_v[...])
        for k in range(CHUNKS):
            wbuf[k, c, b, a, m * PART:(m + 1) * PART, :] = rows[k * PART:(k + 1) * PART].astype(BF16)

    pl.semaphore_wait(barrier, len(everyone))

    def own_start(k):
        block = wbuf.at[k, c, b, a]
        for o in (2, 1, 3):
            send(("a", o, k), block, block, a_to[o])
        for o in (1, 3):
            send(("b", o, 0, k), block, block, b_to[o])

    def slab_start(k):
        for o in (3, 1, 2):
            arrived("a", (4 - o) % 4, k)
            block = wbuf.at[k, c, b, (a + o) % 4]
            for to in (1, 3):
                send(("b", to, o, k), block, block, b_to[to])
        slab = wbuf.at[k, c, b]
        send(("sib0", k), slab, slab, sib)

    def forward(k, to, o):
        arrived("b", to, o, k)
        block = wbuf.at[k, c, (b + 4 - to) % 4, (a + o) % 4]
        send(("f", to, o, k), block, block, b_to[to])

    def slabs_in(k):
        for to in (1, 3):
            for o in ((1, 3) if to == 1 else (0, 2)):
                arrived("b", to, o, k)
            slab = wbuf.at[k, c, (b + 4 - to) % 4]
            send(("sib%d" % to, k), slab, slab, sib)

    def last_slab_in(k):
        for to, o in ((1, 0), (1, 2), (3, 1), (3, 3)):
            arrived("f", to, o, k)
        slab = wbuf.at[k, c, (b + 2) % 4]
        send(("sib2", k), slab, slab, sib)

    def sib_wait(k):
        for i in range(4):
            arrived("sib%d" % i, k)

    def piece(k, m, p, yy, xx):
        at = (k, p, yy, xx) if p == 0 else (k, p, xx, yy)
        return wbuf[at + (slice(m * PART, (m + 1) * PART), slice(None))]

    def wrows(k, m, ys):
        return jnp.concatenate(
            [
                jnp.concatenate([piece(k, m, p, yy, xx) for yy in ys for xx in range(4)], 1)
                for p in range(2)
            ],
            0,
        )

    def hidden_part(k):
        every = range(4)
        w_gu = jnp.concatenate([wrows(k, 0, every), wrows(k, 1, every)], 0)
        gu = dot_nt(xbuf[...], w_gu)
        dh = dot_nt(dybuf[...], wrows(k, 2, every))
        gate, up = gu[:, 0:128], gu[:, 128:256]
        sig = jax.nn.sigmoid(gate)
        hidden = gate * sig * up
        dgate = dh * up * sig * (1.0 + gate * (1.0 - sig))
        dup = dh * gate * sig
        hbuf[:, k * 128:(k + 1) * 128] = hidden.astype(BF16)
        dgubuf[:, k * 256:k * 256 + 128] = dgate.astype(BF16)
        dgubuf[:, k * 256 + 128:(k + 1) * 256] = dup.astype(BF16)
        hT[...] = hidden.T.astype(BF16)
        dguT[0:128, :] = dgate.T.astype(BF16)
        dguT[128:256, :] = dup.T.astype(BF16)

    def grads(k):
        first = len(copies)

        def to_sibling(i):
            bb = (a + 2 - i + (i // 2) * (7 - 2 * i)) % 4
            return bb, remote(first + i, gbuf.at[k, 1 - c, bb], rsib.at[k, bb], sib)

        def body(i, _):
            bb, copy = to_sibling(i)
            where = [(bb + (1 - c) * (n - bb), n + (1 - c) * (bb - n)) for n in range(4)]
            cols = [pl.ds(pl.multiple_of((yy * 4 + xx) * 128, 128), 128) for yy, xx in where]
            g_gu = dot_nn(dguT[...], jnp.concatenate([xbuf[:, at] for at in cols], 1))
            g_d = dot_nn(hT[...], jnp.concatenate([dybuf[:, at] for at in cols], 1))
            for m in range(3):
                for p in range(2):
                    for n, (yy, xx) in enumerate(where):
                        at = (k, p, yy, xx) if p == 0 else (k, p, xx, yy)
                        base = p * PART + (m * 128 if m < 2 else 0)
                        g = (g_gu if m < 2 else g_d)[base:base + PART, n * 128:(n + 1) * 128]
                        gbuf[at + (slice(m * PART, (m + 1) * PART), slice(None))] = g.astype(BF16)
            copy.start()
            return 0

        lax.fori_loop(0, 4, body, 0)
        for i in range(4):
            copies[("gs%d" % i, k)] = to_sibling(i)[1]

    def project(which):
        def body(yy, _):
            cols = pl.ds(pl.multiple_of(yy * 512, 512), 512)
            if which == 0:
                w = jnp.concatenate([wrows(k, 2, [yy]) for k in range(CHUNKS)], 0)
                res = dot_nn(hbuf[...], w)
            else:
                w = jnp.concatenate(
                    [wrows(k, m, [yy]) for k in range(CHUNKS) for m in range(2)], 0
                )
                res = dot_nn(dgubuf[...], w)
            own[which, :, cols] = res[0:ROWS]
            psnd[which, :, cols] = res[ROWS:2 * ROWS].astype(BF16)
            return 0

        lax.fori_loop(0, 4, body, 0)

    def pair_send(which):
        send(("p%d" % which,), psnd.at[which], prcv.at[which], pair)

    def gsum(k, bb, i):
        return gbuf[k, c, bb, i].astype(F32) + rsib[k, bb, i].astype(F32)

    def rb_sum(k, o, lo, hi, more=None):
        def body(i, _):
            total = gsum(k, (b + o) % 4, i)
            if more is not None:
                total = total + brel[k, more, i - lo].astype(F32)
            bsnd[k, o - 1, i] = total.astype(BF16)
            return 0

        lax.fori_loop(lo, hi, body, 0)

    def rb_send(k, o, lo, hi):
        part = slice(lo, hi)
        send(("rb", o, lo, k), bsnd.at[k, o - 1, part], bfin.at[k, o - 1, part], b_to[o])

    def rb_start(k):
        arrived("gs0", k)
        rb_sum(k, 2, 0, 4)
        if k < N_RELAYED:
            send(("rr", 1, k), bsnd.at[k, 1, 0:2], brel.at[k, 0], b_to[1])
            send(("rr", 3, k), bsnd.at[k, 1, 2:4], brel.at[k, 1], b_to[3])
        else:
            rb_send(k, 2, 0, 4)
        for i, o in ((1, 1), (2, 3)):
            arrived("gs%d" % i, k)
            lo, hi = ((2, 4) if o == 1 else (0, 2)) if k < N_RELAYED else (0, 4)
            rb_sum(k, o, lo, hi)
            rb_send(k, o, lo, hi)

    def rb_sent(k):
        if k < N_RELAYED:
            sent(("rr", 1, k), ("rr", 3, k), ("rb", 1, 2, k), ("rb", 3, 0, k))
        else:
            sent(*((("rb", o, 0, k)) for o in (1, 2, 3)))

    def rb_relay(k):
        for n, o in enumerate((1, 3)):
            arrived("rr", o, k)
            lo, hi = (0, 2) if o == 1 else (2, 4)
            rb_sum(k, o, lo, hi, n)
            rb_send(k, o, lo, hi)

    def ra_start(k):
        arrived("gs3", k)
        if k < N_RELAYED:
            waits, terms = [(1, 0), (1, 2), (3, 0), (3, 2)], (1, 3)
        else:
            waits, terms = [(1, 0), (3, 0), (2, 0)], (1, 3, 2)
        for o, lo in waits:
            arrived("rb", o, lo, k)
        for o in (2, 1, 3, 0):
            i = (a + o) % 4
            total = gsum(k, b, i)
            for t in terms:
                total = total + bfin[k, t - 1, i].astype(F32)
            if o:
                asnd[k, o - 1] = total.astype(BF16)
                send(("ra", o, k), asnd.at[k, o - 1], afin.at[k, o - 1], a_to[o])
            else:
                bacc[k] = total

    def ra_final(k):
        blk = bacc[k]
        for o in (1, 3, 2):
            arrived("ra", o, k)
            blk = blk + afin[k, o - 1].astype(F32)
        for t in range(8):
            rows = jnp.concatenate([blk[m * PART + t * 8:m * PART + t * 8 + 8] for m in range(3)], 0)
            zf[k, t] = rows
            zsnd[k, t] = jnp.concatenate([rows, jnp.zeros((8, LANES), F32)], 0).astype(BF16)
        for j in (4, 3, 5, 2, 6, 1, 7):
            send(("z%d" % j, k), zsnd.at[k, (zh + j) % 8], zrcv.at[k, j - 1], peers[j - 1])

    def z_final(k):
        total = zf[k, zh]
        for j in range(1, 8):
            arrived("z%d" % j, k)
            total = total + zrcv[k, j - 1].astype(F32)[0:24]
        total = total * (1.0 / 256.0)
        for m in range(3):
            gr_o[m, k * 8:(k + 1) * 8, :] = total[m * 8:(m + 1) * 8]

    def tile_send():
        send(("tile",), tile, xbuf.at[ROWS:2 * ROWS], pair)

    def dy_send():
        loads[3].wait()
        loads[6].wait()
        kept = lax.broadcasted_iota(jnp.int32, (ROWS, LANES), 1) < valid_s[0]
        spread = jnp.broadcast_to(comb_v[...], (ROWS, LANES))
        weight[0] = jnp.where(kept, spread, 0.0).T
        weight[1] = jnp.where(kept, jnp.ones_like(spread), 0.0).T
        loads[5].wait()
        for s in range(16):
            cols = slice(s * LANES, (s + 1) * LANES)
            dybuf[0:ROWS, cols] = (weight[0] * cot_v[:, cols].astype(F32)).astype(BF16)
        send(("dy",), dybuf.at[0:ROWS], dybuf.at[ROWS:2 * ROWS], pair)

    def rows_wait():
        loads[4].wait()
        arrived("tile")
        arrived("dy")

    stores = [
        pltpu.make_async_copy(fin.at[n], ref, store_sems.at[n]) for n, ref in enumerate((out_o, tg_o))
    ]

    def output_final():
        arrived("p0")

        def body(s, dots):
            cols = pl.ds(pl.multiple_of(s * LANES, LANES), LANES)
            full = own[0, :, cols] + prcv[0, :, cols].astype(F32)
            fin[0, :, cols] = (weight[0] * full).astype(BF16)
            return dots + cot_v[:, cols].astype(F32) * full

        dots = lax.fori_loop(0, 16, body, jnp.zeros((ROWS, LANES), F32))
        stores[0].start()
        total = jnp.broadcast_to(jnp.sum(dots, axis=1, keepdims=True), (ROWS, LANES))
        total = total * weight[1] * (1.0 / math.sqrt(D))
        cg_o[...] = total.T[0:1, :]

    def tile_grad_final():
        arrived("p1")

        def body(s, _):
            cols = pl.ds(pl.multiple_of(s * LANES, LANES), LANES)
            fin[1, :, cols] = (own[1, :, cols] + prcv[1, :, cols].astype(F32)).astype(BF16)
            return 0

        lax.fori_loop(0, 16, body, 0)
        stores[1].start()

    tile_send()
    own_start(0)
    dy_send()
    own_start(1)
    slab_start(0)
    forward(0, 1, 0)
    own_start(2)
    slab_start(1)
    forward(0, 3, 1)
    forward(0, 3, 3)
    forward(0, 1, 2)
    slabs_in(0)
    forward(1, 1, 0)
    slab_start(2)
    last_slab_in(0)
    forward(1, 3, 1)
    forward(1, 3, 3)
    forward(1, 1, 2)
    slabs_in(1)
    forward(2, 1, 0)
    rows_wait()
    sib_wait(0)
    hidden_part(0)
    forward(2, 3, 1)
    forward(2, 3, 3)
    forward(2, 1, 2)
    slabs_in(2)
    last_slab_in(1)
    grads(0)
    sib_wait(1)
    hidden_part(1)
    last_slab_in(2)
    rb_start(0)
    grads(1)
    sib_wait(2)
    hidden_part(2)
    rb_start(1)
    grads(2)
    project(0)
    pair_send(0)
    rb_start(2)
    ra_start(0)
    project(1)
    pair_send(1)
    ra_start(1)
    ra_final(0)
    ra_start(2)
    output_final()
    ra_final(1)
    ra_final(2)
    tile_grad_final()
    for k in range(CHUNKS):
        z_final(k)
    for store in stores:
        store.wait()
    sent(*(name for name in copies if name not in gone))


N_COPIES = (19 + 4 + 6 + 7) * CHUNKS + 3 * N_RELAYED + 4


def on_device(tile, cotangent, combine, valid, w_gate, w_up, w_down):
    vmem = pl.BlockSpec(memory_space=pltpu.VMEM)
    hbm = pl.BlockSpec(memory_space=pltpu.HBM)
    k = CHUNKS
    out, tg, cg, gr = pl.pallas_call(
        kernel,
        out_shape=(
            jax.ShapeDtypeStruct((ROWS, D), BF16),
            jax.ShapeDtypeStruct((ROWS, D), BF16),
            jax.ShapeDtypeStruct((1, ROWS), F32),
            jax.ShapeDtypeStruct((3, 24, LANES), F32),
        ),
        in_specs=[hbm] * 7,
        out_specs=(hbm, hbm, vmem, vmem),
        scratch_shapes=[
            pltpu.VMEM((LANES, FF), BF16),
            pltpu.VMEM((LANES, FF), BF16),
            pltpu.VMEM((FF, LANES), BF16),
            pltpu.VMEM((ROWS, D), BF16),
            pltpu.VMEM((1, ROWS), F32),
            pltpu.SMEM((1,), jnp.int32),
            pltpu.VMEM((k, 2, 4, 4, BLOCK, LANES), BF16),
            pltpu.VMEM((k, 2, 4, 4, BLOCK, LANES), BF16),
            pltpu.VMEM((k, 4, 4, BLOCK, LANES), BF16),
            pltpu.VMEM((2 * ROWS, D), BF16),
            pltpu.VMEM((2 * ROWS, D), BF16),
            pltpu.VMEM((2, ROWS, LANES), F32),
            pltpu.VMEM((2 * ROWS, k * 128), BF16),
            pltpu.VMEM((2 * ROWS, k * 256), BF16),
            pltpu.VMEM((128, 2 * ROWS), BF16),
            pltpu.VMEM((256, 2 * ROWS), BF16),
            pltpu.VMEM((2, ROWS, D), F32),
            pltpu.VMEM((2, ROWS, D), BF16),
            pltpu.VMEM((2, ROWS, D), BF16),
            pltpu.VMEM((2, ROWS, D), BF16),
            pltpu.VMEM((k, 3, 4, BLOCK, LANES), BF16),
            pltpu.VMEM((k, 2, 2, BLOCK, LANES), BF16),
            pltpu.VMEM((k, 3, 4, BLOCK, LANES), BF16),
            pltpu.VMEM((k, BLOCK, LANES), F32),
            pltpu.VMEM((k, 3, BLOCK, LANES), BF16),
            pltpu.VMEM((k, 3, BLOCK, LANES), BF16),
            pltpu.VMEM((k, 8, 24, LANES), F32),
            pltpu.VMEM((k, 8, 32, LANES), BF16),
            pltpu.VMEM((k, 7, 32, LANES), BF16),
            pltpu.SemaphoreType.DMA((7,)),
            pltpu.SemaphoreType.DMA((2,)),
            pltpu.SemaphoreType.DMA((N_COPIES,)),
            pltpu.SemaphoreType.DMA((N_COPIES,)),
        ],
        compiler_params=pltpu.CompilerParams(
            collective_id=0, has_side_effects=True, vmem_limit_bytes=VMEM_BYTES
        ),
        cost_estimate=pl.CostEstimate(
            flops=18 * ROWS * D * FF, bytes_accessed=4 * 1024 * 1024, transcendentals=ROWS * FF
        ),
    )(tile, cotangent, combine.reshape(1, ROWS), valid, w_gate, w_up, w_down)
    grad = jax.ShapeDtypeStruct((24, LANES), F32)
    out, tg, cg, gg, gu, gd = pl.pallas_call(
        hand_over,
        out_shape=(
            jax.ShapeDtypeStruct((ROWS, D), BF16),
            jax.ShapeDtypeStruct((ROWS, D), BF16),
            jax.ShapeDtypeStruct((1, ROWS), F32),
            grad, grad, grad,
        ),
        in_specs=[hbm] * 4,
        out_specs=(hbm,) * 6,
        scratch_shapes=[
            pltpu.VMEM((ROWS, D), BF16),
            pltpu.VMEM((ROWS, D), BF16),
            pltpu.VMEM((1, ROWS), F32),
            pltpu.VMEM((3, 24, LANES), F32),
            pltpu.SemaphoreType.DMA((10,)),
        ],
        compiler_params=pltpu.CompilerParams(vmem_limit_bytes=VMEM_BYTES),
    )(out, tg, cg, gr)
    return (out, tg, cg.reshape(ROWS), gg.T, gu.T, gd)


def solution(mesh):
    in_specs = (
        P(("dp", "fsdp"), None),
        P(("dp", "fsdp"), None),
        P(("dp", "fsdp")),
        P(("dp", "fsdp")),
        P("fsdp", None),
        P("fsdp", None),
        P(None, "fsdp"),
    )
    out_specs = (
        P(("dp", "fsdp"), None),
        P(("dp", "fsdp"), None),
        P(("dp", "fsdp")),
        P("fsdp", "dp"),
        P("fsdp", "dp"),
        P("dp", "fsdp"),
    )
    return jax.shard_map(
        on_device, mesh=mesh, in_specs=in_specs, out_specs=out_specs, check_vma=False
    )
```
